128 devices in a mesh: dp: 4 (over y_lo, core), cent: 32 (over y_hi, x, z).
Axes of the slice: x: 4, y: 4 (y_hi: 2, y_lo: 2; y = y_hi * 2 + y_lo), z: 4, core: 2. Of those that a mesh axis runs over, the one named last changes fastest.
Arguments:
- embeddings: bfloat16 [8192, 1024], P(('dp', 'cent')), may hold values from -3 to 3
- centroids: bfloat16 [65536, 1024], P('cent'), as said below
Outputs:
- assignments: bfloat16 [8192, 65536], P('dp', 'cent')
- counts: float32 [65536], P('cent')
- centroids_next: bfloat16 [1024, 65536], P('dp', 'cent')
The draws below stay inside these ranges and needn't reach their ends.
Inputs may be any that keep to these rules, and one draw needn't show every extreme that they name: `centroids`: every entry has magnitude at most 6 / sqrt(1024).
All inputs are finite; a program needn't handle non-finite values.
Results may differ from the reference program's by a relative error of at most 0.014.
Values may be sent and summed in bfloat16 or wider, within the bound.
No kernel may reach another device: no remote copies, remote signals or barrier semaphores. Data moves between devices by JAX's collectives and lax.ppermute only.
A program may use at most 128 MiB of HBM per device.

```python
import math
import jax
import jax.numpy as jnp
from jax import lax

D = 1024
R_DEV = 64
GROUP = 2048
N = 8192
K = 65536
N_DP = 4
N_CENT = 32


def centroid_signs(key, index):
    bits = jax.random.bernoulli(jax.random.fold_in(key, index), 0.5, (D,))
    return jnp.where(bits, 1.0, -1.0).astype(jnp.float32)


def centroid_level(key, index, lower, upper):
    inner = jax.random.fold_in(jax.random.fold_in(key, 11), index)
    return jnp.exp(jax.random.uniform(inner, (), jnp.float32, jnp.log(lower), jnp.log(upper)))


def group_rise(spread):
    groups = N // GROUP
    index = (jnp.arange(N) // GROUP).astype(jnp.float32)
    return (1.0 + spread * index / max(groups - 1, 1))[:, None]


def draw_centroids(key, part):
    indices = jnp.arange(K, dtype=jnp.int32)
    broad = jax.vmap(lambda i: centroid_level(key, i, 1.0, 6.0))(indices)
    scales = broad
    signs = jax.vmap(lambda i: centroid_signs(key, i))(indices)
    values = signs * (scales / jnp.sqrt(float(D)))[:, None]
    return values.astype(jnp.bfloat16)


def draw_embeddings(key, part):
    shared = key
    key = jax.random.fold_in(key, 5)
    keys = jax.random.split(key, 8)
    scale = jnp.exp(jax.random.uniform(keys[0], (N, 1), jnp.float32, jnp.log(0.016), jnp.log(0.16)))
    scale = scale * group_rise(2.0)
    values = scale * jnp.clip(jax.random.normal(keys[2], (N, D), jnp.float32), -5.0, 5.0)
    targets = jax.random.randint(keys[6], (N,), 0, K)
    lift = jax.random.uniform(keys[7], (N,), jnp.float32, 10.0, 20.0)
    target_scale = jax.vmap(lambda i: centroid_level(shared, i, 1.0, 6.0))(targets)
    target_level = (target_scale / jnp.sqrt(float(D))).astype(jnp.bfloat16).astype(jnp.float32)
    target_signs = jax.vmap(lambda i: centroid_signs(shared, i))(targets)
    values = values + (lift / (2.0 * D * target_level))[:, None] * target_signs
    return values.astype(jnp.bfloat16)


def setup_inputs(seed: int = 0) -> dict:
    seeds = jax.random.split(jax.random.key(seed), 3)
    embeddings = draw_embeddings(jax.random.fold_in(seeds[2], 71), 0)
    centroids = draw_centroids(jax.random.fold_in(seeds[2], 71), 0)
    return {"embeddings": embeddings, "centroids": centroids}


TEMP_INV = 2.0
PRIOR = 0.05


def soft_block(rows, centroids):
    logits = jnp.dot(rows, centroids.T, preferred_element_type=jnp.float32) * TEMP_INV
    peak = jnp.max(logits, axis=1, keepdims=True)
    total = jnp.sum(jnp.exp(logits - peak), axis=1, keepdims=True)
    lse = peak + jnp.log(total)
    return jnp.exp(logits - lse).astype(jnp.bfloat16)


def reference(embeddings, centroids):
    group = R_DEV * N_CENT
    block = math.gcd(group, 512)
    blocked = embeddings.reshape(N // block, block, D)
    assigned = lax.map(lambda rows: soft_block(rows, centroids), blocked)
    assignments = assigned.reshape(N, K)
    sums = jnp.zeros((D, K), jnp.float32)
    counts = jnp.zeros((K,), jnp.float32)
    for index in range(N_DP):
        rows = embeddings[index * group:(index + 1) * group]
        weights = assignments[index * group:(index + 1) * group]
        partial_sum = jnp.dot(rows.T, weights, preferred_element_type=jnp.float32)
        sums = sums + partial_sum.astype(jnp.bfloat16).astype(jnp.float32)
        counts = counts + jnp.sum(weights.astype(jnp.float32), axis=0)
    previous = centroids.astype(jnp.float32).T
    centroids_next = ((sums + PRIOR * previous) / (counts + PRIOR)[None, :]).astype(jnp.bfloat16)
    return assignments, counts, centroids_next
```

```python
import functools
import math

import jax
import jax.numpy as jnp
from jax import lax
from jax.experimental import pallas as pl
from jax.experimental.pallas import tpu as pltpu
from jax.sharding import PartitionSpec as P

TEMP_INV = 2.0
PRIOR = 0.05
SCALE = TEMP_INV * math.log2(math.e)
AXES = ("dp", "cent")
VMEM = pl.BlockSpec(memory_space=pltpu.VMEM)
SMEM = pl.BlockSpec(memory_space=pltpu.SMEM)
ANY = pl.BlockSpec(memory_space=pl.ANY)
LIMIT = 40 * 2**20
TILE = 256


def _perm(move):
    pairs = []
    for dp in range(4):
        for cent in range(32):
            core = dp & 1
            yh, x, z = cent >> 4, (cent >> 2) & 3, cent & 3
            first, second = (x, z) if core == 0 else (z, x)
            yh2, first, second = move(yh, first, second)
            x2, z2 = (first, second) if core == 0 else (second, first)
            pairs.append((dp * 32 + cent, dp * 32 + (yh2 % 2) * 16 + (x2 % 4) * 4 + z2 % 4))
    return pairs


def _first(k):
    return _perm(lambda h, a, b: (h, a + k, b))


def _second(k):
    return _perm(lambda h, a, b: (h, a, b + k))


FAR = _perm(lambda h, a, b: (h + 1, a, b))
CORE = [(i, i ^ 1) for i in range(4)]
NEAR = [(i, i ^ 2) for i in range(4)]


def _send(value, pairs):
    return lax.ppermute(value, AXES, pairs)


def _soft_body(e_ref, c_ref, p_ref, peak_ref, part_ref, lg):
    for i in range(e_ref.shape[0] // TILE):
        rows = pl.ds(i * TILE, TILE)
        e = e_ref[rows, :]
        top = None
        for j in range(4):
            part = lax.dot_general(
                e, c_ref[j * 512:(j + 1) * 512, :], (((1,), (1,)), ((), ())),
                preferred_element_type=jnp.float32,
            )
            lg[:, j * 512:(j + 1) * 512] = part
            for q in range(4):
                piece = part[:, q * 128:(q + 1) * 128]
                top = piece if top is None else jnp.maximum(top, piece)
        peak = jnp.max(top, axis=1, keepdims=True)
        total = None
        for j in range(16):
            cols = slice(j * 128, (j + 1) * 128)
            value = jnp.exp2((lg[:, cols] - peak) * SCALE)
            total = value if total is None else total + value
            p_ref[rows, cols] = value
        total = jnp.sum(total, axis=1, keepdims=True)
        peak = jnp.transpose(jnp.broadcast_to(peak * SCALE, (TILE, 128)))
        total = jnp.transpose(jnp.broadcast_to(total, (TILE, 128)))
        for q in range(TILE // 128):
            row = pl.ds(i * (TILE // 128) + q, 1)
            peak_ref[row, :] = peak[:1, q * 128:(q + 1) * 128]
            part_ref[row, :] = peak[:1, q * 128:(q + 1) * 128] + jnp.log2(
                total[:1, q * 128:(q + 1) * 128]
            )


def _soft(e, c):
    rows = e.shape[0]
    stat = jax.ShapeDtypeStruct((rows // 128, 128), jnp.float32)
    return pl.pallas_call(
        _soft_body,
        out_shape=(jax.ShapeDtypeStruct((rows, 2048), jnp.float32), stat, stat),
        in_specs=[VMEM, VMEM],
        out_specs=(VMEM, VMEM, VMEM),
        scratch_shapes=[pltpu.VMEM((TILE, 2048), jnp.float32)],
        compiler_params=pltpu.CompilerParams(vmem_limit_bytes=LIMIT),
        cost_estimate=pl.CostEstimate(
            flops=2 * rows * 2048 * 1024, bytes_accessed=rows * 2048 * 4, transcendentals=rows * 2048
        ),
        name="soft",
    )(e, c)


def _assign_body(p0, p1, p2, p3, scale_ref, a_ref, mass_ref):
    mass = [jnp.zeros((8, 128), jnp.float32) for _ in range(16)]
    for g in range(16):
        p_ref = (p0, p1, p2, p3)[g // 4]
        scale = jnp.transpose(jnp.broadcast_to(scale_ref[g:g + 1, :], (128, 128)))
        for j in range(16):
            cols = slice(j * 128, (j + 1) * 128)
            value = (p_ref[(g % 4) * 128:(g % 4 + 1) * 128, cols] * scale).astype(jnp.bfloat16)
            a_ref[g * 128:(g + 1) * 128, cols] = value
            mass[j] = mass[j] + jnp.sum(value.astype(jnp.float32).reshape(16, 8, 128), axis=0)
    for j in range(16):
        mass_ref[:, j * 128:(j + 1) * 128] = jnp.sum(mass[j], axis=0, keepdims=True)


def _assign(pieces, scale):
    return pl.pallas_call(
        _assign_body,
        out_shape=(
            jax.ShapeDtypeStruct((2048, 2048), jnp.bfloat16),
            jax.ShapeDtypeStruct((1, 2048), jnp.float32),
        ),
        in_specs=[VMEM] * 5,
        out_specs=(VMEM, VMEM),
        compiler_params=pltpu.CompilerParams(vmem_limit_bytes=LIMIT),
        name="assign",
    )(*pieces, scale)


def _sums_body(offset_ref, e_ref, a_ref, out_ref):
    e = e_ref[:, pl.ds(pl.multiple_of(offset_ref[0], 256), 256)]
    for j in range(4):
        cols = slice(j * 512, (j + 1) * 512)
        out_ref[:, cols] = lax.dot_general(
            e, a_ref[:, cols], (((0,), (0,)), ((), ())), preferred_element_type=jnp.float32
        ).astype(out_ref.dtype)


def _sums(offset, e, a):
    return pl.pallas_call(
        _sums_body,
        out_shape=jax.ShapeDtypeStruct((256, 2048), jnp.bfloat16),
        in_specs=[SMEM, VMEM, VMEM],
        out_specs=VMEM,
        compiler_params=pltpu.CompilerParams(vmem_limit_bytes=LIMIT),
        cost_estimate=pl.CostEstimate(
            flops=2 * 256 * 2048 * 2048, bytes_accessed=2**23, transcendentals=0
        ),
        name="sums",
    )(offset.reshape(1), e, a)


def _place_body(where_ref, a_ref, out_ref, sem):
    copies = [
        pltpu.make_async_copy(
            a_ref.at[pl.ds(i * 64, 64)],
            out_ref.at[pl.ds(pl.multiple_of(where_ref[i] * 64, 64), 64)],
            sem.at[i],
        )
        for i in range(32)
    ]
    for copy in copies:
        copy.start()
    for copy in copies:
        copy.wait()


def _place(where, a):
    return pl.pallas_call(
        _place_body,
        out_shape=jax.ShapeDtypeStruct(a.shape, a.dtype),
        in_specs=[SMEM, ANY],
        out_specs=ANY,
        scratch_shapes=[pltpu.SemaphoreType.DMA((32,))],
        name="place",
    )(where, a)


def _merge(values):
    top = functools.reduce(jnp.maximum, values)
    return top + jnp.log2(sum(jnp.exp2(v - top) for v in values))


def _row_total(part):
    near = part.reshape(4, 4, 128)
    near = _merge([near] + [
        jnp.roll(_send(part, _first(-k)).reshape(4, 4, 128), k, axis=1) for k in (1, -1, 2)
    ])
    part = near.reshape(16, 128)
    wide = part.reshape(4, 512)
    wide = _merge([wide] + [
        jnp.roll(_send(part, _second(-k)).reshape(4, 512), k, axis=0) for k in (1, -1, 2)
    ])
    part = wide.reshape(16, 128)
    return _merge([part, jnp.roll(_send(part, FAR), 64, axis=1)])


def on_device(embeddings, centroids):
    dp, cent = lax.axis_index("dp"), lax.axis_index("cent")
    near, core = dp // 2, dp % 2
    far, x, z = cent // 16, (cent // 4) % 4, cent % 4

    e0 = jnp.concatenate([embeddings, _send(embeddings, FAR)])
    e0 = jnp.concatenate([e0] + [_send(e0, _first(-k)) for k in (1, 2, 3)])
    e1, e3 = _send(e0, _second(-1)), _send(e0, _second(1))
    e2 = jnp.concatenate([_send(e3[:256], _second(1)), _send(e1[256:], _second(-1))])
    pieces = [_soft(e, centroids) for e in (e0, e1, e2, e3)]
    rows = jnp.concatenate([e0, e1, e2, e3])

    peak = jnp.concatenate([p[1] for p in pieces])
    total = _row_total(jnp.concatenate([p[2] for p in pieces]))
    assigned, mass = _assign([p[0] for p in pieces], jnp.exp2(peak - total))

    width = 256
    away, home = (1 - near) * 2, near * 2
    arrived = lax.ppermute(_sums((away + 1 - core) * width, rows, assigned), "dp", CORE)
    kept = _sums((away + core) * width, rows, assigned)
    outgoing = (kept.astype(jnp.float32) + arrived.astype(jnp.float32)).astype(jnp.bfloat16)
    incoming = lax.ppermute(outgoing, "dp", NEAR)
    arrived = lax.ppermute(_sums((home + 1 - core) * width, rows, assigned), "dp", CORE)
    kept = _sums((home + core) * width, rows, assigned)
    mass = mass + lax.ppermute(mass, "dp", CORE)
    mass = mass + lax.ppermute(mass, "dp", NEAR)

    index = jnp.arange(32)
    b, a, h = index // 8, (index // 2) % 4, index % 2
    px = (x + jnp.where(core == 0, a, b)) % 4
    pz = (z + jnp.where(core == 0, b, a)) % 4
    where = (far ^ h) * 16 + px * 4 + pz
    placed = _place(where.astype(jnp.int32), assigned)

    previous = lax.dynamic_slice_in_dim(centroids, dp * width, width, 1).astype(jnp.float32).T
    sums = kept.astype(jnp.float32) + arrived.astype(jnp.float32) + incoming.astype(jnp.float32)
    centroids_next = ((sums + PRIOR * previous) / (mass + PRIOR)).astype(jnp.bfloat16)
    return placed, mass.reshape(2048), centroids_next


def solution(mesh):
    placed = (P(("dp", "cent"), None), P("cent", None))
    return jax.shard_map(
        on_device,
        mesh=mesh,
        in_specs=placed,
        out_specs=(P("dp", "cent"), P("cent"), P("dp", "cent")),
        check_vma=False,
    )
```

```python
import functools
import math

import jax
import jax.numpy as jnp
from jax import lax
from jax.experimental import pallas as pl
from jax.experimental.pallas import tpu as pltpu
from jax.sharding import PartitionSpec as P

TEMP_INV = 2.0
PRIOR = 0.05
SCALE = TEMP_INV * math.log2(math.e)
AXES = ("dp", "cent")
VMEM = pl.BlockSpec(memory_space=pltpu.VMEM)
ANY = pl.BlockSpec(memory_space=pl.ANY)
LIMIT = 10 * 2**20
F32, BF16 = jnp.float32, jnp.bfloat16


def _perm(move):
    pairs = []
    for dp in range(4):
        for cent in range(32):
            core = dp & 1
            far, x, z = cent >> 4, (cent >> 2) & 3, cent & 3
            first, second = (x, z) if core == 0 else (z, x)
            far, first, second = move(far, first, second)
            x, z = (first, second) if core == 0 else (second, first)
            pairs.append((dp * 32 + cent, dp * 32 + (far % 2) * 16 + (x % 4) * 4 + z % 4))
    return pairs


def _first(k):
    return _perm(lambda h, a, b: (h, a + k, b))


def _second(k):
    return _perm(lambda h, a, b: (h, a, b + k))


FAR = _perm(lambda h, a, b: (h + 1, a, b))
CORE = [(i, i ^ 1) for i in range(4)]
NEAR = [(i, i ^ 2) for i in range(4)]


def _send(value, pairs):
    return lax.ppermute(value, AXES, pairs)


def _kernel(body, outs, inputs, name, flops=0, moved=0, exps=0, scratch=(), out_specs=None):
    return pl.pallas_call(
        body,
        out_shape=outs,
        in_specs=[VMEM] * len(inputs),
        out_specs=out_specs if out_specs is not None else jax.tree.map(lambda _: VMEM, outs),
        scratch_shapes=list(scratch),
        compiler_params=pltpu.CompilerParams(vmem_limit_bytes=LIMIT),
        cost_estimate=pl.CostEstimate(flops=flops, bytes_accessed=moved, transcendentals=exps),
        name=name,
    )(*inputs)


def _shape(*dims, dtype=BF16):
    return jax.ShapeDtypeStruct(dims, dtype)


def _place_of(a, b):
    core, cent = lax.axis_index("dp") & 1, lax.axis_index("cent")
    x, z = (cent >> 2) & 3, cent & 3
    first = (jnp.where(core == 0, x, z) + a) & 3
    second = (jnp.where(core == 0, z, x) + b) & 3
    return jnp.where(core == 0, first, second) * 4 + jnp.where(core == 0, second, first)


def _swap_far(row):
    return jnp.where(lax.axis_index("cent") >= 16, pltpu.roll(row, 64, axis=1), row)


def _join_body(*refs):
    start = 0
    for ref in refs[:-1]:
        refs[-1][start:start + ref.shape[0], :] = ref[...]
        start += ref.shape[0]


def _join(*parts):
    rows = sum(p.shape[0] for p in parts)
    return _kernel(_join_body, _shape(rows, parts[0].shape[1]), parts, "join", moved=rows * 4096)


def _soft_body(n, *refs):
    e_refs, c_ref, p_refs, (peak_ref, part_ref, lg) = refs[:n], refs[n], refs[n + 1:2 * n + 1], refs[2 * n + 1:]
    for i in range(n):
        e = e_refs[i][...]
        top = None
        for j in range(4):
            part = lax.dot_general(
                e, c_ref[j * 512:(j + 1) * 512, :], (((1,), (1,)), ((), ())),
                preferred_element_type=F32,
            )
            lg[:, j * 512:(j + 1) * 512] = part
            for q in range(4):
                piece = part[:, q * 128:(q + 1) * 128]
                top = piece if top is None else jnp.maximum(top, piece)
        peak = jnp.max(top, axis=1, keepdims=True)
        total = None
        for j in range(16):
            cols = slice(j * 128, (j + 1) * 128)
            value = jnp.exp2((lg[:, cols] - peak) * SCALE)
            total = value if total is None else total + value
            p_refs[i][:, cols] = value
        total = jnp.sum(total, axis=1, keepdims=True)
        peak = jnp.transpose(jnp.broadcast_to(peak * SCALE, (256, 128)))
        total = jnp.transpose(jnp.broadcast_to(total, (256, 128)))
        for q in range(2):
            lanes = slice(q * 128, (q + 1) * 128)
            row = slice(i * 2 + q, i * 2 + q + 1)
            peak_ref[row, :] = peak[:1, lanes]
            part_ref[row, :] = peak[:1, lanes] + jnp.log2(total[:1, lanes])


def _soft(pieces, c):
    n = len(pieces)
    stat = _shape(2 * n, 128, dtype=F32)
    outs = _kernel(
        functools.partial(_soft_body, n), [_shape(256, 2048, dtype=F32)] * n + [stat, stat], [*pieces, c], "soft",
        flops=n * 2**30, exps=n * 2**19, scratch=[pltpu.VMEM((256, 2048), F32)],
    )
    return outs[:n], outs[n], outs[n + 1]


def _pack_body(places, *refs):
    for ref, slots in zip(refs[:-1], places):
        for i, (a, b) in enumerate(slots):
            refs[-1][pl.ds(_place_of(a, b), 1), :] = _swap_far(ref[i:i + 1, :])


def _pack(parts, places):
    return _kernel(functools.partial(_pack_body, places), _shape(16, 128, dtype=F32), parts, "pack")


def _merge_body(*refs):
    values = [r[...] for r in refs[:-1]]
    top = functools.reduce(jnp.maximum, values)
    refs[-1][...] = top + jnp.log2(sum(jnp.exp2(v - top) for v in values))


def _merge(*values):
    return _kernel(_merge_body, _shape(16, 128, dtype=F32), values, "merge")


def _add_body(a_ref, b_ref, out_ref):
    out_ref[...] = (a_ref[...].astype(F32) + b_ref[...].astype(F32)).astype(out_ref.dtype)


def _add(a, b):
    return _kernel(_add_body, _shape(*a.shape, dtype=a.dtype), [a, b], "add")


def _flip_body(*refs):
    for i, ref in enumerate(refs[:-1]):
        refs[-1][:, i * 256:(i + 1) * 256] = jnp.transpose(ref[...])


def _flip(pieces):
    return _kernel(_flip_body, _shape(1024, 2048), pieces, "flip", moved=2**22)


def _rows_of(et_ref, home):
    dp = lax.axis_index("dp")
    near, core = dp >> 1, dp & 1
    base = (near if home else 1 - near) * 512
    sent = et_ref[pl.ds(pl.multiple_of(base + (1 - core) * 256, 256), 256), :]
    kept = et_ref[pl.ds(pl.multiple_of(base + core * 256, 256), 256), :]
    return [sent, kept]


def _assign_body(start, width, places, *refs):
    p_refs, (n0, n1, n2, n3, total_ref, et_ref, a_ref, sent_ref, kept_ref, mass_ref) = refs[:8], refs[8:]
    for g in range(16):
        call, i, a, b = places[g]
        peak = (n0, n1, n2, n3)[call][i:i + 1, :]
        row = _swap_far(total_ref[pl.ds(_place_of(a, b), 1), :])
        scale = jnp.transpose(jnp.broadcast_to(jnp.exp2(peak - row), (128, 128)))
        for j in range(width // 128):
            cols = slice(start + j * 128, start + (j + 1) * 128)
            value = p_refs[g // 2][(g % 2) * 128:(g % 2 + 1) * 128, cols] * scale
            a_ref[g * 128:(g + 1) * 128, j * 128:(j + 1) * 128] = value.astype(BF16)
    rows = jnp.concatenate(_rows_of(et_ref, False) + [jnp.ones((16, 2048), BF16)], axis=0)
    for n in range(width // 512):
        cols = slice(n * 512, (n + 1) * 512)
        out = jnp.dot(rows, a_ref[:, cols], preferred_element_type=F32)
        sent_ref[:, cols] = out[:256].astype(BF16)
        kept_ref[:, cols] = out[256:512].astype(BF16)
        mass_ref[:, cols] = out[512:513]


def _assign(start, width, places, ps, peaks, total, et):
    return _kernel(
        functools.partial(_assign_body, start, width, places),
        [_shape(2048, width), _shape(256, width), _shape(256, width), _shape(1, width, dtype=F32)],
        [*ps, *peaks, total, et], "assign", flops=2**21 * width, moved=2**12 * width,
    )


def _home_body(et_ref, a0, a1, m0, m1, sent_ref, kept_ref, mass_ref):
    rows = jnp.concatenate(_rows_of(et_ref, True), axis=0)
    for n in range(4):
        cols = slice(n * 512, (n + 1) * 512)
        half = slice((n % 2) * 512, (n % 2 + 1) * 512)
        out = jnp.dot(rows, (a0, a1)[n // 2][:, half], preferred_element_type=F32)
        sent_ref[:, cols] = out[:256].astype(BF16)
        kept_ref[:, cols] = out[256:].astype(BF16)
    mass_ref[:, :1024] = m0[...]
    mass_ref[:, 1024:] = m1[...]


def _home(et, a0, a1, m0, m1):
    return _kernel(
        _home_body, [_shape(256, 2048), _shape(256, 2048), _shape(1, 2048, dtype=F32)],
        [et, a0, a1, m0, m1], "home", flops=2**32, moved=2**23,
    )


def _place_body(a0, a1, out_ref, sem):
    far = lax.axis_index("cent") >> 4
    copies = []
    for i in range(32):
        b, a, h = i // 8, (i // 2) % 4, i % 2
        row = pl.multiple_of(((far ^ h) * 16 + _place_of(a, b)) * 64, 64)
        for n, ref in enumerate((a0, a1)):
            copies.append(pltpu.make_async_copy(
                ref.at[pl.ds(i * 64, 64)], out_ref.at[pl.ds(row, 64), pl.ds(n * 1024, 1024)], sem.at[2 * i + n]
            ))
    for copy in copies:
        copy.start()
    for copy in copies:
        copy.wait()


def _place(a0, a1):
    return _kernel(
        _place_body, _shape(2048, 2048), [a0, a1], "place", moved=2**24,
        scratch=[pltpu.SemaphoreType.DMA((64,))], out_specs=ANY,
    )


def _base_body(kept_ref, arrived_ref, c_ref, out_ref):
    dp = lax.axis_index("dp")
    previous = jnp.transpose(c_ref[:, pl.ds(pl.multiple_of(dp * 256, 256), 256)])
    out_ref[...] = kept_ref[...].astype(F32) + arrived_ref[...].astype(F32) + PRIOR * previous.astype(F32)


def _base(kept, arrived, c):
    return _kernel(_base_body, _shape(256, 2048, dtype=F32), [kept, arrived, c], "base", moved=2**22)


def _final_body(base_ref, in0, in1, mass_ref, out_ref):
    for n, ref in enumerate((in0, in1)):
        cols = slice(n * 1024, (n + 1) * 1024)
        out_ref[:, cols] = ((base_ref[:, cols] + ref[...].astype(F32)) / (mass_ref[:, cols] + PRIOR)).astype(BF16)


def _final(base, in0, in1, mass):
    return _kernel(_final_body, _shape(256, 2048), [base, in0, in1, mass], "final", moved=2**22)


def on_device(embeddings, centroids):
    start = _join(embeddings, _send(embeddings, FAR))
    one, two, three = (_send(start, _first(-k)) for k in (1, 2, 3))
    e0a, e0b = _join(start, one), _join(two, three)
    e3a, e1b = _send(e0a, _second(1)), _send(e0b, _second(-1))
    e3b, e1a = _send(e0b, _second(1)), _send(e0a, _second(-1))
    e2a, e2b = _send(e3a, _second(1)), _send(e1b, _second(-1))

    calls = [[(0, 0, e0a), (0, 1, e0b)], [(3, 0, e3a), (1, 1, e1b)], [(3, 1, e3b), (1, 0, e1a)], [(2, 0, e2a), (2, 1, e2b)]]
    pieces, probs, where, peaks, parts, slots = {}, {}, {}, [], [], []
    for n, call in enumerate(calls):
        p, peak, part = _soft([e for _, _, e in call], centroids)
        for i, (b, half, e) in enumerate(call):
            pieces[b, half], probs[b, half] = e, p[i]
            for q in range(2):
                where[b, half, q] = (n, 2 * i + q, 2 * half + q, b)
        peaks.append(peak)
        parts.append(part)
        slots.append([(2 * half + q, b) for b, half, _ in call for q in range(2)])
    order = [(b, half) for b in range(4) for half in range(2)]
    where = [where[b, half, q] for b, half in order for q in range(2)]

    part = _pack(parts, slots)
    et = _flip([pieces[k] for k in order])
    part = _merge(part, *(_send(part, _first(k)) for k in (1, 2, 3)))
    part = _merge(part, *(_send(part, _second(k)) for k in (1, 2, 3)))
    total = _merge(part, _send(part, FAR))

    ps = [probs[k] for k in order]
    a0, sent, kept, m0 = _assign(0, 1024, where, ps, peaks, total, et)
    out0 = _add(kept, lax.ppermute(sent, "dp", CORE))
    out0, total = lax.optimization_barrier((out0, total))
    in0 = lax.ppermute(out0, "dp", NEAR)
    a1, sent, kept, m1 = _assign(1024, 1024, where, ps, peaks, total, et)
    out1 = _add(kept, lax.ppermute(sent, "dp", CORE))
    out1, a1 = lax.optimization_barrier((out1, a1))
    in1 = lax.ppermute(out1, "dp", NEAR)

    sent, kept, mass = _home(et, a0, a1, m0, m1)
    arrived = lax.ppermute(sent, "dp", CORE)
    mass = _add(mass, lax.ppermute(mass, "dp", CORE))
    mass = _add(mass, lax.ppermute(mass, "dp", NEAR))
    base = _base(kept, arrived, centroids)
    placed = _place(a0, a1)
    return placed, mass.reshape(2048), _final(base, in0, in1, mass)


def solution(mesh):
    placed = (P(("dp", "cent"), None), P("cent", None))
    return jax.shard_map(
        on_device,
        mesh=mesh,
        in_specs=placed,
        out_specs=(P("dp", "cent"), P("cent"), P("dp", "cent")),
        check_vma=False,
    )
```

```python
import functools
import math

import jax
import jax.numpy as jnp
from jax import lax
from jax.experimental import pallas as pl
from jax.experimental.pallas import tpu as pltpu
from jax.sharding import PartitionSpec as P

TEMP_INV = 2.0
PRIOR = 0.05
SCALE = TEMP_INV * math.log2(math.e)
AXES = ("dp", "cent")
VMEM = pl.BlockSpec(memory_space=pltpu.VMEM)
HBM = pl.BlockSpec(memory_space=pltpu.HBM)
LIMIT = 16 * 2**20
F32, BF16 = jnp.float32, jnp.bfloat16


def _perm(move):
    pairs = []
    for dp in range(4):
        for cent in range(32):
            core = dp & 1
            far, x, z = cent >> 4, (cent >> 2) & 3, cent & 3
            first, second = (x, z) if core == 0 else (z, x)
            far, first, second = move(far, first, second)
            x, z = (first, second) if core == 0 else (second, first)
            pairs.append((dp * 32 + cent, dp * 32 + (far % 2) * 16 + (x % 4) * 4 + z % 4))
    return pairs


def _first(k):
    return _perm(lambda h, a, b: (h, a + k, b))


def _second(k):
    return _perm(lambda h, a, b: (h, a, b + k))


FAR = _perm(lambda h, a, b: (h + 1, a, b))
CORE = [(i, i ^ 1) for i in range(4)]
NEAR = [(i, i ^ 2) for i in range(4)]


def _send(value, pairs):
    return lax.ppermute(value, AXES, pairs)


def _shape(*dims, dtype=BF16):
    return jax.ShapeDtypeStruct(dims, dtype)


def _kernel(body, outs, inputs, name, scratch=(), hbm_in=(), hbm_out=(), aliases=None, limit=LIMIT, flops=0):
    return pl.pallas_call(
        body,
        out_shape=outs,
        in_specs=[HBM if i in hbm_in else VMEM for i in range(len(inputs))],
        out_specs=[HBM if i in hbm_out else VMEM for i in range(len(outs))],
        scratch_shapes=list(scratch),
        input_output_aliases=aliases or {},
        compiler_params=pltpu.CompilerParams(vmem_limit_bytes=limit),
        cost_estimate=pl.CostEstimate(flops=flops, bytes_accessed=0, transcendentals=0) if flops else None,
        name=name,
    )(*inputs)


def _place_of(a, b):
    core, cent = lax.axis_index("dp") & 1, lax.axis_index("cent")
    x, z = (cent >> 2) & 3, cent & 3
    first = (jnp.where(core == 0, x, z) + a) & 3
    second = (jnp.where(core == 0, z, x) + b) & 3
    return jnp.where(core == 0, first, second) * 4 + jnp.where(core == 0, second, first)


def _far():
    return lax.axis_index("cent") >> 4


def _swap_far(row):
    return jnp.where(_far() == 0, row, pltpu.roll(row, 64, axis=1))


def _join_body(*refs):
    start = 0
    for ref in refs[:-1]:
        refs[-1][start:start + ref.shape[0], :] = ref[...]
        start += ref.shape[0]


def _join(*parts):
    rows = sum(p.shape[0] for p in parts)
    return _kernel(_join_body, [_shape(rows, 1024)], parts, "join")[0]


def _load_body(e_in, c_ref, e_ref, previous_ref):
    e_ref[...] = e_in[...]
    width = previous_ref.shape[0]
    offset = pl.multiple_of(lax.axis_index("dp") * width, width)
    previous_ref[...] = jnp.transpose(c_ref[:, pl.ds(offset, width)])


def _load(e, c):
    return _kernel(_load_body, [_shape(*e.shape), _shape(256, 2048)], [e, c], "load")


def _soft_body(n, slots, first, *refs):
    e_refs, c_ref, refs = refs[:n], refs[n], refs[n + (1 if first else 2):]
    p_refs, (peak_ref, part_ref, et_ref, lg) = refs[:n], refs[n:]
    for i in range(n):
        e = e_refs[i][...]
        et_ref[:, slots[i] * 256:(slots[i] + 1) * 256] = jnp.transpose(e)
        top = None
        for j in range(4):
            part = lax.dot_general(
                e, c_ref[j * 512:(j + 1) * 512, :], (((1,), (1,)), ((), ())),
                preferred_element_type=F32,
            )
            lg[:, j * 512:(j + 1) * 512] = part
            for q in range(4):
                piece = part[:, q * 128:(q + 1) * 128]
                top = piece if top is None else jnp.maximum(top, piece)
        peak = jnp.max(top, axis=1, keepdims=True)
        total = None
        for j in range(16):
            cols = slice(j * 128, (j + 1) * 128)
            value = jnp.exp2((lg[:, cols] - peak) * SCALE)
            total = value if total is None else total + value
            p_refs[i][:, cols] = value
        total = jnp.sum(total, axis=1, keepdims=True)
        peak = jnp.transpose(jnp.broadcast_to(peak * SCALE, (256, 128)))
        total = jnp.transpose(jnp.broadcast_to(total, (256, 128)))
        for q in range(2):
            lanes = slice(q * 128, (q + 1) * 128)
            row = slice(i * 2 + q, i * 2 + q + 1)
            peak_ref[row, :] = peak[:1, lanes]
            part_ref[row, :] = peak[:1, lanes] + jnp.log2(total[:1, lanes])


def _soft(pieces, slots, c, et):
    n, first = len(pieces), et is None
    stat = _shape(2 * n, 128, dtype=F32)
    outs = [_shape(256, 2048, dtype=F32)] * n + [stat, stat, _shape(1024, 2048)]
    scratch = [pltpu.VMEM((256, 2048), F32)]
    body = functools.partial(_soft_body, n, slots, first)
    inputs, aliases = ([*pieces, c], None) if first else ([*pieces, c, et], {n + 1: n + 2})
    outs = _kernel(body, outs, inputs, "soft", scratch=scratch, aliases=aliases)
    return outs[:n], outs[n], outs[n + 1], outs[n + 2]


def _pack_body(where, *refs):
    out_ref, one = refs[-2], refs[-1]
    for b in range(4):
        for a in range(4):
            call, i = where[b * 4 + a]
            one[pl.ds(_place_of(a, b), 1), :] = _swap_far(refs[call][i:i + 1, :])
    packed = one[...]
    for i in range(32):
        out_ref[i] = packed


def _pack(parts, where):
    return _kernel(
        functools.partial(_pack_body, where), [_shape(32, 16, 128, dtype=F32)], parts, "pack",
        scratch=[pltpu.VMEM((16, 128), F32)],
    )[0]


def _merge_body(in_ref, out_ref):
    values = [in_ref[i] for i in range(32)]
    top = functools.reduce(jnp.maximum, values)
    out_ref[...] = top + jnp.log2(sum(jnp.exp2(v - top) for v in values))


def _merge(values):
    return _kernel(_merge_body, [_shape(16, 128, dtype=F32)], [values], "merge")[0]


def _copy_body(in_ref, out_ref):
    out_ref[...] = in_ref[...]


def _copy(value):
    return _kernel(_copy_body, [_shape(*value.shape)], [value], "copy", flops=2**36)[0]


def _sum_rows(et_ref, home):
    dp = lax.axis_index("dp")
    near, core = dp >> 1, dp & 1
    base = (near if home else 1 - near) * 512
    sent = et_ref[pl.ds(pl.multiple_of(base + (1 - core) * 256, 256), 256), :]
    kept = et_ref[pl.ds(pl.multiple_of(base + core * 256, 256), 256), :]
    return [sent, kept]


def _assign_part(where, start, width, p_refs, peaks, total_ref, a_ref, placed_ref, sem):
    copies = []
    for g in range(16):
        call, i = where[g]
        place = _place_of(g % 4, g // 4)
        row = peaks[call][i:i + 1, :] - _swap_far(total_ref[pl.ds(place, 1), :])
        scale = jnp.transpose(jnp.broadcast_to(jnp.exp2(row), (128, 128)))
        for j in range(width // 128):
            value = p_refs[g // 2][g % 2 * 128:(g % 2 + 1) * 128, start + j * 128:start + (j + 1) * 128] * scale
            a_ref[g * 128:(g + 1) * 128, j * 128:(j + 1) * 128] = value.astype(BF16)
        for t in range(2):
            row = pl.multiple_of(((_far() ^ t) * 16 + place) * 64, 64)
            copy = pltpu.make_async_copy(
                a_ref.at[pl.ds(g * 128 + t * 64, 64)],
                placed_ref.at[pl.ds(row, 64), pl.ds(start, width)],
                sem.at[2 * g + t],
            )
            copy.start()
            copies.append(copy)
    return copies


def _assign_body(where, width, calls, *refs):
    p_refs, peaks, refs = refs[:8], refs[8:8 + calls], refs[8 + calls:]
    total_ref, et_ref, a_ref, placed_ref, sent_ref, kept_ref, mass_ref, sem = refs
    copies = _assign_part(where, 0, width, p_refs, peaks, total_ref, a_ref, placed_ref, sem)
    rows = jnp.concatenate(_sum_rows(et_ref, False) + [jnp.ones((16, 2048), BF16)], axis=0)
    for n in range(width // 256):
        cols = slice(n * 256, (n + 1) * 256)
        out = jnp.dot(rows, a_ref[:, cols], preferred_element_type=F32)
        sent_ref[:, cols] = out[:256].astype(BF16)
        kept_ref[:, cols] = out[256:512].astype(BF16)
        mass_ref[:, cols] = out[512:513]
    for copy in copies:
        copy.wait()


def _assign(where, width, ps, peaks, total, et):
    return _kernel(
        functools.partial(_assign_body, where, width, len(peaks)),
        [_shape(2048, width), _shape(2048, 2048), _shape(256, width), _shape(256, width), _shape(1, width, dtype=F32)],
        [*ps, *peaks, total, et], "assign", scratch=[pltpu.SemaphoreType.DMA((32,))], hbm_out=(1,),
    )


def _rest_body(where, width, calls, n, *refs):
    p_refs, peaks, refs = refs[:8], refs[8:8 + calls], refs[8 + calls:]
    total_ref, et_ref, m0, _, placed_ref, a_ref = refs[:6]
    sent_refs, (kept_ref, mass_ref, sem) = refs[6:6 + n], refs[6 + n:]
    left = 2048 - width
    copies = _assign_part(where, width, left, p_refs, peaks, total_ref, a_ref, placed_ref, sem)
    rows = jnp.concatenate(_sum_rows(et_ref, False) + [jnp.ones((16, 2048), BF16)], axis=0)
    for j in range(left // 256):
        cols = slice(j * 256, (j + 1) * 256)
        out = jnp.dot(rows, a_ref[:, cols], preferred_element_type=F32)
        step = left // n
        sent_refs[j * 256 // step][:, j * 256 % step:j * 256 % step + 256] = out[:256].astype(BF16)
        kept_ref[:, cols] = out[256:512].astype(BF16)
        mass_ref[:, width + j * 256:width + (j + 1) * 256] = out[512:513]
    mass_ref[:, :width] = m0[...]
    for copy in copies:
        copy.wait()


def _rest(where, width, n, ps, peaks, total, et, m0, placed):
    left = 2048 - width
    inputs = [*ps, *peaks, total, et, m0, placed]
    outs = _kernel(
        functools.partial(_rest_body, where, width, len(peaks), n),
        [_shape(2048, 2048), _shape(2048, left)] + [_shape(256, left // n)] * n
        + [_shape(256, left), _shape(1, 2048, dtype=F32)],
        inputs, "rest", scratch=[pltpu.SemaphoreType.DMA((32,))],
        hbm_in=(len(inputs) - 1,), hbm_out=(0,), aliases={len(inputs) - 1: 0},
    )
    return outs[0], outs[1], outs[2:2 + n], outs[2 + n], outs[3 + n]


def _home_body(et_ref, a0, a1, sent_ref, kept_ref):
    rows = jnp.concatenate(_sum_rows(et_ref, True), axis=0)
    start = 0
    for a_ref in (a0, a1):
        for j in range(a_ref.shape[1] // 256):
            cols = slice(start + j * 256, start + (j + 1) * 256)
            out = jnp.dot(rows, a_ref[:, j * 256:(j + 1) * 256], preferred_element_type=F32)
            sent_ref[:, cols] = out[:256].astype(BF16)
            kept_ref[:, cols] = out[256:].astype(BF16)
        start += a_ref.shape[1]


def _home(*inputs):
    return _kernel(_home_body, [_shape(256, 2048), _shape(256, 2048)], inputs, "home", flops=1)


def _fold_body(kept_ref, *refs):
    start = 0
    for ref in refs[:-1]:
        cols = slice(start, start + ref.shape[1])
        start += ref.shape[1]
        refs[-1][:, cols] = (kept_ref[:, cols].astype(F32) + ref[...].astype(F32)).astype(BF16)


def _fold(kept, *sent):
    return _kernel(_fold_body, [_shape(*kept.shape)], [kept, *sent], "fold", flops=1)[0]


def _fold_mass_body(mass_ref, other_ref, *refs):
    _fold_body(*refs[:-1])
    refs[-1][...] = mass_ref[...] + other_ref[...]


def _fold_mass(mass, other, kept, *sent):
    outs = [_shape(*kept.shape), _shape(1, 2048, dtype=F32)]
    return _kernel(_fold_mass_body, outs, [mass, other, kept, *sent], "fold", flops=1)


def _final_body(in0, in1, home_ref, sent_ref, previous_ref, mass_ref, other_ref, out_ref, total_ref):
    total_ref[...] = mass_ref[...] + other_ref[...]
    start = 0
    for ref in (in0, in1):
        cols = slice(start, start + ref.shape[1])
        start += ref.shape[1]
        sums = home_ref[:, cols].astype(F32) + sent_ref[:, cols].astype(F32) + ref[...].astype(F32)
        sums = sums + PRIOR * previous_ref[:, cols].astype(F32)
        out_ref[:, cols] = (sums / (total_ref[:, cols] + PRIOR)).astype(BF16)


def _final(*inputs):
    return _kernel(_final_body, [_shape(256, 2048), _shape(1, 2048, dtype=F32)], inputs, "final")


def on_device(embeddings, centroids):
    width = 1024
    other = _send(embeddings, FAR)
    own = [embeddings] + [_send(embeddings, _first(-k)) for k in (1, 2, 3)]
    other = [other] + [_send(other, _first(-k)) for k in (1, 2, 3)]
    c = centroids
    e, previous = _load(embeddings, centroids)
    own[2], e = lax.optimization_barrier((own[2], e))
    own[0] = e
    e0a = _join(own[0], other[0], own[1], other[1])
    e0b = _join(own[2], other[2], own[3], other[3])
    e3a, e1b = _send(e0a, _second(1)), _send(e0b, _second(-1))
    calls = [_soft([e0a, e0b], (0, 1), c, None)]
    e0a, e0b, et = lax.optimization_barrier((e0a, e0b, calls[0][3]))
    e3b, e1a = _send(e0b, _second(1)), _send(e0a, _second(-1))
    e3a, e1b, et = lax.optimization_barrier((e3a, e1b, et))
    e2a, e2b = _send(e3a, _second(1)), _send(e1b, _second(-1))
    calls.append(_soft([e3a, e1b], (6, 3), c, et))
    calls.append(_soft([e3b, e1a], (7, 2), c, calls[1][3]))
    calls.append(_soft([e2a, e2b], (4, 5), c, calls[2][3]))
    et = calls[3][3]

    probs, where = [None] * 8, [None] * 16
    for n, (call, slots) in enumerate(zip(calls, ((0, 1), (6, 3), (7, 2), (4, 5)))):
        for i, slot in enumerate(slots):
            probs[slot] = call[0][i]
            where[2 * slot], where[2 * slot + 1] = (n, 2 * i), (n, 2 * i + 1)
    peaks = [call[1] for call in calls]
    parts = _pack([call[2] for call in calls], where)
    total = _merge(lax.all_to_all(parts, "cent", 0, 0).reshape(32, 16, 128))

    a0, placed, sent, kept, m0 = _assign(where, width, probs, peaks, total, et)
    out0 = _fold(kept, lax.ppermute(sent, "dp", CORE))
    out0, total = lax.optimization_barrier((out0, total))
    in0 = lax.ppermute(out0, "dp", NEAR)
    placed, a1, sent, kept, mass = _rest(where, width, 2, probs, peaks, total, et, m0, placed)
    other_mass = lax.ppermute(mass, "dp", CORE)
    out1, mass = _fold_mass(mass, other_mass, kept, *(lax.ppermute(part, "dp", CORE) for part in sent))
    in1 = _copy(lax.ppermute(out1, "dp", NEAR))
    a0, out1 = lax.optimization_barrier((a0, out1))
    sent, kept = _home(et, a0, a1)
    in0, sent = lax.optimization_barrier((_copy(in0), sent))
    sent = lax.ppermute(sent, "dp", CORE)
    result, mass = _final(in0, in1, kept, sent, previous, mass, lax.ppermute(mass, "dp", NEAR))
    return placed, mass.reshape(2048), result


def solution(mesh):
    placed = (P(("dp", "cent"), None), P("cent", None))
    return jax.shard_map(
        on_device,
        mesh=mesh,
        in_specs=placed,
        out_specs=(P("dp", "cent"), P("cent"), P("dp", "cent")),
        check_vma=False,
    )
```

```python
import functools
import math

import jax
import jax.numpy as jnp
from jax import lax
from jax.experimental import pallas as pl
from jax.experimental.pallas import tpu as pltpu
from jax.sharding import PartitionSpec as P

TEMP_INV = 2.0
PRIOR = 0.05
SCALE = TEMP_INV * math.log2(math.e)
AXES = ("dp", "cent")
VMEM = pl.BlockSpec(memory_space=pltpu.VMEM)
HBM = pl.BlockSpec(memory_space=pltpu.HBM)
HEAD, REST = (768,), (512, 512, 256)
LIMIT = 16 * 2**20
F32, BF16 = jnp.float32, jnp.bfloat16


def _perm(move):
    pairs = []
    for dp in range(4):
        for cent in range(32):
            core = dp & 1
            far, x, z = cent >> 4, (cent >> 2) & 3, cent & 3
            first, second = (x, z) if core == 0 else (z, x)
            far, first, second = move(far, first, second)
            x, z = (first, second) if core == 0 else (second, first)
            pairs.append((dp * 32 + cent, dp * 32 + (far % 2) * 16 + (x % 4) * 4 + z % 4))
    return pairs


def _first(k):
    return _perm(lambda h, a, b: (h, a + k, b))


def _second(k):
    return _perm(lambda h, a, b: (h, a, b + k))


FAR = _perm(lambda h, a, b: (h + 1, a, b))
CORE = [(i, i ^ 1) for i in range(4)]
NEAR = [(i, i ^ 2) for i in range(4)]


def _send(value, pairs):
    return lax.ppermute(value, AXES, pairs)


def _shape(*dims, dtype=BF16):
    return jax.ShapeDtypeStruct(dims, dtype)


def _kernel(body, outs, inputs, name, scratch=(), hbm_in=(), hbm_out=(), aliases=None, limit=LIMIT, flops=0):
    return pl.pallas_call(
        body,
        out_shape=outs,
        in_specs=[HBM if i in hbm_in else VMEM for i in range(len(inputs))],
        out_specs=[HBM if i in hbm_out else VMEM for i in range(len(outs))],
        scratch_shapes=list(scratch),
        input_output_aliases=aliases or {},
        compiler_params=pltpu.CompilerParams(vmem_limit_bytes=limit),
        cost_estimate=pl.CostEstimate(flops=flops, bytes_accessed=0, transcendentals=0) if flops else None,
        name=name,
    )(*inputs)


def _place_of(a, b):
    core, cent = lax.axis_index("dp") & 1, lax.axis_index("cent")
    x, z = (cent >> 2) & 3, cent & 3
    first = (jnp.where(core == 0, x, z) + a) & 3
    second = (jnp.where(core == 0, z, x) + b) & 3
    return jnp.where(core == 0, first, second) * 4 + jnp.where(core == 0, second, first)


def _far():
    return lax.axis_index("cent") >> 4


def _swap_far(row):
    return jnp.where(_far() == 0, row, pltpu.roll(row, 64, axis=1))


def _join_body(*refs):
    start = 0
    for ref in refs[:-1]:
        refs[-1][start:start + ref.shape[0], :] = ref[...]
        start += ref.shape[0]


def _join(*parts):
    rows = sum(p.shape[0] for p in parts)
    return _kernel(_join_body, [_shape(rows, 1024)], parts, "join")[0]


def _soft_body(n, slots, first, *refs):
    e_refs, c_ref, refs = refs[:n], refs[n], refs[n + (1 if first else 2):]
    p_refs, (peak_ref, part_ref, et_ref, *previous, lg) = refs[:n], refs[n:]
    if first:
        width = previous[0].shape[0]
        offset = pl.multiple_of(lax.axis_index("dp") * width, width)
        previous[0][...] = jnp.transpose(c_ref[:, pl.ds(offset, width)])
    for i in range(n):
        e = e_refs[i][...]
        et_ref[:, slots[i] * 256:(slots[i] + 1) * 256] = jnp.transpose(e)
        top = None
        for j in range(4):
            part = lax.dot_general(
                e, c_ref[j * 512:(j + 1) * 512, :], (((1,), (1,)), ((), ())),
                preferred_element_type=F32,
            )
            lg[:, j * 512:(j + 1) * 512] = part
            for q in range(4):
                piece = part[:, q * 128:(q + 1) * 128]
                top = piece if top is None else jnp.maximum(top, piece)
        peak = jnp.max(top, axis=1, keepdims=True)
        total = None
        for j in range(16):
            cols = slice(j * 128, (j + 1) * 128)
            value = jnp.exp2((lg[:, cols] - peak) * SCALE)
            total = value if total is None else total + value
            p_refs[i][:, cols] = value
        total = jnp.sum(total, axis=1, keepdims=True)
        peak = jnp.transpose(jnp.broadcast_to(peak * SCALE, (256, 128)))
        total = jnp.transpose(jnp.broadcast_to(total, (256, 128)))
        for q in range(2):
            lanes = slice(q * 128, (q + 1) * 128)
            row = slice(i * 2 + q, i * 2 + q + 1)
            peak_ref[row, :] = peak[:1, lanes]
            part_ref[row, :] = peak[:1, lanes] + jnp.log2(total[:1, lanes])


def _soft(pieces, slots, c, et):
    n, first = len(pieces), et is None
    stat = _shape(2 * n, 128, dtype=F32)
    outs = [_shape(256, 2048, dtype=F32)] * n + [stat, stat, _shape(1024, 2048)]
    scratch = [pltpu.VMEM((256, 2048), F32)]
    body = functools.partial(_soft_body, n, slots, first)
    inputs, aliases = ([*pieces, c], None) if first else ([*pieces, c, et], {n + 1: n + 2})
    if first:
        outs.append(_shape(256, 2048))
    outs = _kernel(body, outs, inputs, "soft", scratch=scratch, aliases=aliases)
    return outs[:n], outs[n], outs[n + 1], outs[n + 2], outs[n + 3:]


def _pack_body(where, *refs):
    out_ref, one = refs[-2], refs[-1]
    for b in range(4):
        for a in range(4):
            call, i = where[b * 4 + a]
            one[pl.ds(_place_of(a, b), 1), :] = _swap_far(refs[call][i:i + 1, :])
    packed = one[...]
    for i in range(32):
        out_ref[i] = packed


def _pack(parts, where):
    return _kernel(
        functools.partial(_pack_body, where), [_shape(32, 16, 128, dtype=F32)], parts, "pack",
        scratch=[pltpu.VMEM((16, 128), F32)],
    )[0]


def _merge_body(in_ref, out_ref):
    values = [in_ref[i] for i in range(32)]
    top = functools.reduce(jnp.maximum, values)
    out_ref[...] = top + jnp.log2(sum(jnp.exp2(v - top) for v in values))


def _merge(values):
    return _kernel(_merge_body, [_shape(16, 128, dtype=F32)], [values], "merge")[0]


def _copy_body(in_ref, out_ref):
    out_ref[...] = in_ref[...]


def _copy(value):
    return _kernel(_copy_body, [_shape(*value.shape)], [value], "copy", flops=2**36)[0]


def _sum_rows(et_ref, home):
    dp = lax.axis_index("dp")
    near, core = dp >> 1, dp & 1
    base = (near if home else 1 - near) * 512
    sent = et_ref[pl.ds(pl.multiple_of(base + (1 - core) * 256, 256), 256), :]
    kept = et_ref[pl.ds(pl.multiple_of(base + core * 256, 256), 256), :]
    return [sent, kept]


def _assign_dot(where, start, width, p_refs, peaks, total_ref, scale_ref, a_ref, rows, store):
    for g in range(16):
        call, i = where[g]
        row = peaks[call][i:i + 1, :] - _swap_far(total_ref[pl.ds(_place_of(g % 4, g // 4), 1), :])
        scale_ref[g * 128:(g + 1) * 128, :] = jnp.transpose(jnp.broadcast_to(jnp.exp2(row), (128, 128)))
    for n in range(width // 256):
        for g in range(16):
            scale = scale_ref[g * 128:(g + 1) * 128, :]
            for j in range(2 * n, 2 * n + 2):
                value = p_refs[g // 2][g % 2 * 128:(g % 2 + 1) * 128, start + j * 128:start + (j + 1) * 128]
                a_ref[g * 128:(g + 1) * 128, j * 128:(j + 1) * 128] = (value * scale).astype(BF16)
        cols = slice(n * 256, (n + 1) * 256)
        store(n, cols, jnp.dot(rows, a_ref[:, cols], preferred_element_type=F32))


def _assign_body(where, start, width, parts, calls, *refs):
    p_refs, peaks, refs = refs[:8], refs[8:8 + calls], refs[8 + calls:]
    total_ref, et_ref = refs[:2]
    mass_in = refs[2] if start else None
    a_ref, *refs = refs[3:] if start else refs[2:]
    sent_refs, (kept_ref, mass_ref, scale_ref) = refs[:len(parts)], refs[len(parts):]
    rows = jnp.concatenate(_sum_rows(et_ref, False) + [jnp.ones((16, 2048), BF16)], axis=0)

    def store(n, cols, out):
        first, part = n * 256, 0
        while first >= parts[part]:
            first, part = first - parts[part], part + 1
        sent_refs[part][:, first:first + 256] = out[:256].astype(BF16)
        kept_ref[:, cols] = out[256:512].astype(BF16)
        mass_ref[:, start + n * 256:start + (n + 1) * 256] = out[512:513]

    _assign_dot(where, start, width, p_refs, peaks, total_ref, scale_ref, a_ref, rows, store)
    if start:
        mass_ref[:, :start] = mass_in[...]


def _assign(where, start, parts, ps, peaks, total, et, *mass):
    width, n = sum(parts), len(parts)
    outs = _kernel(
        functools.partial(_assign_body, where, start, width, parts, len(peaks)),
        [_shape(2048, width)] + [_shape(256, part) for part in parts]
        + [_shape(256, width), _shape(1, start + width, dtype=F32)],
        [*ps, *peaks, total, et, *mass], "assign", scratch=[pltpu.VMEM((2048, 128), F32)],
    )
    return outs[0], outs[1:1 + n], outs[1 + n], outs[2 + n]


def _home_body(et_ref, a0, a1, sent_ref, kept_ref, placed_ref, sem):
    copies = []
    for i in range(32):
        row = pl.multiple_of(((_far() ^ (i % 2)) * 16 + _place_of(i // 2 % 4, i // 8)) * 64, 64)
        start = 0
        for n, a_ref in enumerate((a0, a1)):
            copies.append(pltpu.make_async_copy(
                a_ref.at[pl.ds(i * 64, 64)],
                placed_ref.at[pl.ds(row, 64), pl.ds(start, a_ref.shape[1])],
                sem.at[2 * i + n],
            ))
            start += a_ref.shape[1]
    for copy in copies:
        copy.start()
    rows = jnp.concatenate(_sum_rows(et_ref, True), axis=0)
    start = 0
    for a_ref in (a0, a1):
        for j in range(a_ref.shape[1] // 256):
            cols = slice(start + j * 256, start + (j + 1) * 256)
            out = jnp.dot(rows, a_ref[:, j * 256:(j + 1) * 256], preferred_element_type=F32)
            sent_ref[:, cols] = out[:256].astype(BF16)
            kept_ref[:, cols] = out[256:].astype(BF16)
        start += a_ref.shape[1]
    for copy in copies:
        copy.wait()


def _home(*inputs):
    return _kernel(
        _home_body, [_shape(256, 2048), _shape(256, 2048), _shape(2048, 2048)], inputs, "home",
        scratch=[pltpu.SemaphoreType.DMA((64,))], hbm_out=(2,), flops=1,
    )


def _fold_body(kept_ref, *refs):
    start = 0
    for ref in refs[:-1]:
        cols = slice(start, start + ref.shape[1])
        start += ref.shape[1]
        refs[-1][:, cols] = (kept_ref[:, cols].astype(F32) + ref[...].astype(F32)).astype(BF16)


def _fold(kept, *sent):
    return _kernel(_fold_body, [_shape(*kept.shape)], [kept, *sent], "fold", flops=1)[0]


def _fold_mass_body(mass_ref, other_ref, *refs):
    _fold_body(*refs[:-1])
    refs[-1][...] = mass_ref[...] + other_ref[...]


def _fold_mass(mass, other, kept, *sent):
    outs = [_shape(*kept.shape), _shape(1, 2048, dtype=F32)]
    return _kernel(_fold_mass_body, outs, [mass, other, kept, *sent], "fold", flops=1)


def _final_body(in0, in1, home_ref, sent_ref, previous_ref, mass_ref, other_ref, out_ref, total_ref):
    total_ref[...] = mass_ref[...] + other_ref[...]
    start = 0
    for ref in (in0, in1):
        cols = slice(start, start + ref.shape[1])
        start += ref.shape[1]
        inverse = 1.0 / (total_ref[:, cols] + PRIOR)
        sums = home_ref[:, cols].astype(F32) + sent_ref[:, cols].astype(F32) + ref[...].astype(F32)
        out_ref[:, cols] = ((sums + PRIOR * previous_ref[:, cols].astype(F32)) * inverse).astype(BF16)


def _final(*inputs):
    return _kernel(_final_body, [_shape(256, 2048), _shape(1, 2048, dtype=F32)], inputs, "final")


def on_device(embeddings, centroids):
    other = _copy(_send(embeddings, FAR))
    own = [embeddings] + [_send(embeddings, _first(-k)) for k in (1, 2, 3)]
    other = [other] + [_send(other, _first(-k)) for k in (1, 2, 3)]
    c = centroids
    own, other = lax.optimization_barrier((own, other))
    e0a = _join(own[0], other[0], own[1], other[1])
    e0b = _join(own[2], other[2], own[3], other[3])
    e3b, e1a = _send(e0b, _second(1)), _send(e0a, _second(-1))
    e3a, e1b = _send(e0a, _second(1)), _send(e0b, _second(-1))
    calls = [_soft([e0a, e0b], (0, 1), c, None)]
    previous, et = calls[0][4][0], calls[0][3]
    e3b, e1a, et = lax.optimization_barrier((e3b, e1a, et))
    e2b, e2a = _send(e3b, _second(1)), _send(e1a, _second(-1))
    calls.append(_soft([e3b, e1a], (7, 2), c, et))
    calls.append(_soft([e3a, e1b], (6, 3), c, calls[1][3]))
    calls.append(_soft([e2a, e2b], (4, 5), c, calls[2][3]))
    et = calls[3][3]

    probs, where = [None] * 8, [None] * 16
    for n, (call, slots) in enumerate(zip(calls, ((0, 1), (7, 2), (6, 3), (4, 5)))):
        for i, slot in enumerate(slots):
            probs[slot] = call[0][i]
            where[2 * slot], where[2 * slot + 1] = (n, 2 * i), (n, 2 * i + 1)
    peaks = [call[1] for call in calls]
    parts = _pack([call[2] for call in calls], where)
    total = _merge(lax.all_to_all(parts, "cent", 0, 0).reshape(32, 16, 128))

    a0, sent, kept, mass = _assign(where, 0, HEAD, probs, peaks, total, et)
    out0 = _fold(kept, *(lax.ppermute(part, "dp", CORE) for part in sent))
    out0, total = lax.optimization_barrier((out0, total))
    in0 = lax.ppermute(out0, "dp", NEAR)
    a1, sent, kept, mass = _assign(where, sum(HEAD), REST, probs, peaks, total, et, mass)
    other_mass = lax.ppermute(mass, "dp", CORE)
    out1, mass = _fold_mass(mass, other_mass, kept, *(lax.ppermute(part, "dp", CORE) for part in sent))
    in1 = _copy(lax.ppermute(out1, "dp", NEAR))
    a0, out1 = lax.optimization_barrier((a0, out1))
    sent, kept, placed = _home(et, a0, a1)
    in0, sent = lax.optimization_barrier((_copy(in0), sent))
    sent = lax.ppermute(sent, "dp", CORE)
    result, mass = _final(in0, in1, kept, sent, previous, mass, lax.ppermute(mass, "dp", NEAR))
    return placed, mass.reshape(2048), result


def solution(mesh):
    placed = (P(("dp", "cent"), None), P("cent", None))
    return jax.shard_map(
        on_device,
        mesh=mesh,
        in_specs=placed,
        out_specs=(P("dp", "cent"), P("cent"), P("dp", "cent")),
        check_vma=False,
    )
```

```python
import functools
import math

import jax
import jax.numpy as jnp
from jax import lax
from jax.experimental import pallas as pl
from jax.experimental.pallas import tpu as pltpu
from jax.sharding import PartitionSpec as P

TEMP_INV = 2.0
PRIOR = 0.05
SCALE = TEMP_INV * math.log2(math.e)
AXES = ("dp", "cent")
VMEM = pl.BlockSpec(memory_space=pltpu.VMEM)
HBM = pl.BlockSpec(memory_space=pltpu.HBM)
HEAD, REST = (768,), (512, 512, 256)
LIMIT = 16 * 2**20
F32, BF16 = jnp.float32, jnp.bfloat16


def _perm(move):
    pairs = []
    for dp in range(4):
        for cent in range(32):
            core = dp & 1
            far, x, z = cent >> 4, (cent >> 2) & 3, cent & 3
            first, second = (z, x) if core == 0 else (x, z)
            far, first, second = move(far, first, second)
            x, z = (second, first) if core == 0 else (first, second)
            pairs.append((dp * 32 + cent, dp * 32 + (far % 2) * 16 + (x % 4) * 4 + z % 4))
    return pairs


def _first(k):
    return _perm(lambda h, a, b: (h, a + k, b))


def _second(k):
    return _perm(lambda h, a, b: (h, a, b + k))


FAR = _perm(lambda h, a, b: (h + 1, a, b))
CORE = [(i, i ^ 1) for i in range(4)]
NEAR = [(i, i ^ 2) for i in range(4)]


def _send(value, pairs):
    return lax.ppermute(value, AXES, pairs)


def _shape(*dims, dtype=BF16):
    return jax.ShapeDtypeStruct(dims, dtype)


def _kernel(body, outs, inputs, name, scratch=(), hbm_in=(), hbm_out=(), aliases=None, limit=LIMIT, flops=0):
    return pl.pallas_call(
        body,
        out_shape=outs,
        in_specs=[HBM if i in hbm_in else VMEM for i in range(len(inputs))],
        out_specs=[HBM if i in hbm_out else VMEM for i in range(len(outs))],
        scratch_shapes=list(scratch),
        input_output_aliases=aliases or {},
        compiler_params=pltpu.CompilerParams(vmem_limit_bytes=limit),
        cost_estimate=pl.CostEstimate(flops=flops, bytes_accessed=0, transcendentals=0) if flops else None,
        name=name,
    )(*inputs)


def _place_of(a, b):
    core, cent = lax.axis_index("dp") & 1, lax.axis_index("cent")
    x, z = (cent >> 2) & 3, cent & 3
    first = (jnp.where(core == 0, z, x) + a) & 3
    second = (jnp.where(core == 0, x, z) + b) & 3
    return jnp.where(core == 0, second, first) * 4 + jnp.where(core == 0, first, second)


def _far():
    return lax.axis_index("cent") >> 4


def _swap_far(row):
    return jnp.where(_far() == 0, row, pltpu.roll(row, 64, axis=1))


def _join_body(*refs):
    start = 0
    for ref in refs[:-1]:
        refs[-1][start:start + ref.shape[0], :] = ref[...]
        start += ref.shape[0]


def _join(*parts):
    rows = sum(p.shape[0] for p in parts)
    return _kernel(_join_body, [_shape(rows, 1024)], parts, "join")[0]


def _soft_body(n, slots, first, *refs):
    e_refs, c_ref, refs = refs[:n], refs[n], refs[n + (1 if first else 2):]
    p_refs, (peak_ref, part_ref, et_ref, *previous, lg) = refs[:n], refs[n:]
    if first:
        width = previous[0].shape[0]
        offset = pl.multiple_of(lax.axis_index("dp") * width, width)
        previous[0][...] = jnp.transpose(c_ref[:, pl.ds(offset, width)])
    for i in range(n):
        e = e_refs[i][...]
        et_ref[:, slots[i] * 256:(slots[i] + 1) * 256] = jnp.transpose(e)
        top = None
        for j in range(4):
            part = lax.dot_general(
                e, c_ref[j * 512:(j + 1) * 512, :], (((1,), (1,)), ((), ())),
                preferred_element_type=F32,
            )
            lg[:, j * 512:(j + 1) * 512] = part
            for q in range(4):
                piece = part[:, q * 128:(q + 1) * 128]
                top = piece if top is None else jnp.maximum(top, piece)
        peak = jnp.max(top, axis=1, keepdims=True)
        total = None
        for j in range(16):
            cols = slice(j * 128, (j + 1) * 128)
            value = jnp.exp2((lg[:, cols] - peak) * SCALE)
            total = value if total is None else total + value
            p_refs[i][:, cols] = value
        total = jnp.sum(total, axis=1, keepdims=True)
        peak = jnp.transpose(jnp.broadcast_to(peak * SCALE, (256, 128)))
        total = jnp.transpose(jnp.broadcast_to(total, (256, 128)))
        for q in range(2):
            lanes = slice(q * 128, (q + 1) * 128)
            row = slice(i * 2 + q, i * 2 + q + 1)
            peak_ref[row, :] = peak[:1, lanes]
            part_ref[row, :] = peak[:1, lanes] + jnp.log2(total[:1, lanes])


def _soft(pieces, slots, c, et):
    n, first = len(pieces), et is None
    stat = _shape(2 * n, 128, dtype=F32)
    outs = [_shape(256, 2048, dtype=F32)] * n + [stat, stat, _shape(1024, 2048)]
    scratch = [pltpu.VMEM((256, 2048), F32)]
    body = functools.partial(_soft_body, n, slots, first)
    inputs, aliases = ([*pieces, c], None) if first else ([*pieces, c, et], {n + 1: n + 2})
    if first:
        outs.append(_shape(256, 2048))
    outs = _kernel(body, outs, inputs, "soft", scratch=scratch, aliases=aliases)
    return outs[:n], outs[n], outs[n + 1], outs[n + 2], outs[n + 3:]


def _pack_body(where, *refs):
    out_ref, one = refs[-2], refs[-1]
    for b in range(4):
        for a in range(4):
            call, i = where[b * 4 + a]
            one[pl.ds(_place_of(a, b), 1), :] = _swap_far(refs[call][i:i + 1, :])
    packed = one[...]
    for i in range(32):
        out_ref[i] = packed


def _pack(parts, where):
    return _kernel(
        functools.partial(_pack_body, where), [_shape(32, 16, 128, dtype=F32)], parts, "pack",
        scratch=[pltpu.VMEM((16, 128), F32)],
    )[0]


def _merge_body(in_ref, out_ref):
    values = [in_ref[i] for i in range(32)]
    top = functools.reduce(jnp.maximum, values)
    out_ref[...] = top + jnp.log2(sum(jnp.exp2(v - top) for v in values))


def _merge(values):
    return _kernel(_merge_body, [_shape(16, 128, dtype=F32)], [values], "merge")[0]


def _copy_body(in_ref, out_ref):
    out_ref[...] = in_ref[...]


def _copy(value):
    return _kernel(_copy_body, [_shape(*value.shape)], [value], "copy", flops=2**36)[0]


def _sum_rows(et_ref, home):
    dp = lax.axis_index("dp")
    near, core = dp >> 1, dp & 1
    base = (near if home else 1 - near) * 512
    sent = et_ref[pl.ds(pl.multiple_of(base + (1 - core) * 256, 256), 256), :]
    kept = et_ref[pl.ds(pl.multiple_of(base + core * 256, 256), 256), :]
    return [sent, kept]


def _assign_dot(where, start, width, p_refs, peaks, total_ref, scale_ref, a_ref, rows, store):
    for g in range(16):
        call, i = where[g]
        row = peaks[call][i:i + 1, :] - _swap_far(total_ref[pl.ds(_place_of(g % 4, g // 4), 1), :])
        scale_ref[g * 128:(g + 1) * 128, :] = jnp.transpose(jnp.broadcast_to(jnp.exp2(row), (128, 128)))
    for n in range(width // 256):
        for g in range(16):
            scale = scale_ref[g * 128:(g + 1) * 128, :]
            for j in range(2 * n, 2 * n + 2):
                value = p_refs[g // 2][g % 2 * 128:(g % 2 + 1) * 128, start + j * 128:start + (j + 1) * 128]
                a_ref[g * 128:(g + 1) * 128, j * 128:(j + 1) * 128] = (value * scale).astype(BF16)
        cols = slice(n * 256, (n + 1) * 256)
        store(n, cols, jnp.dot(rows, a_ref[:, cols], preferred_element_type=F32))


def _assign_body(where, start, width, parts, calls, *refs):
    p_refs, peaks, refs = refs[:8], refs[8:8 + calls], refs[8 + calls:]
    total_ref, et_ref = refs[:2]
    mass_in = refs[2] if start else None
    a_ref, *refs = refs[3:] if start else refs[2:]
    sent_refs, (kept_ref, mass_ref, scale_ref) = refs[:len(parts)], refs[len(parts):]
    rows = jnp.concatenate(_sum_rows(et_ref, False) + [jnp.ones((16, 2048), BF16)], axis=0)

    def store(n, cols, out):
        first, part = n * 256, 0
        while first >= parts[part]:
            first, part = first - parts[part], part + 1
        sent_refs[part][:, first:first + 256] = out[:256].astype(BF16)
        kept_ref[:, cols] = out[256:512].astype(BF16)
        mass_ref[:, start + n * 256:start + (n + 1) * 256] = out[512:513]

    _assign_dot(where, start, width, p_refs, peaks, total_ref, scale_ref, a_ref, rows, store)
    if start:
        mass_ref[:, :start] = mass_in[...]


def _assign(where, start, parts, ps, peaks, total, et, *mass):
    width, n = sum(parts), len(parts)
    outs = _kernel(
        functools.partial(_assign_body, where, start, width, parts, len(peaks)),
        [_shape(2048, width)] + [_shape(256, part) for part in parts]
        + [_shape(256, width), _shape(1, start + width, dtype=F32)],
        [*ps, *peaks, total, et, *mass], "assign", scratch=[pltpu.VMEM((2048, 128), F32)],
    )
    return outs[0], outs[1:1 + n], outs[1 + n], outs[2 + n]


def _home_body(et_ref, a0, a1, sent_ref, kept_ref, placed_ref, sem):
    copies = []
    for i in range(32):
        row = pl.multiple_of(((_far() ^ (i % 2)) * 16 + _place_of(i // 2 % 4, i // 8)) * 64, 64)
        start = 0
        for n, a_ref in enumerate((a0, a1)):
            copies.append(pltpu.make_async_copy(
                a_ref.at[pl.ds(i * 64, 64)],
                placed_ref.at[pl.ds(row, 64), pl.ds(start, a_ref.shape[1])],
                sem.at[2 * i + n],
            ))
            start += a_ref.shape[1]
    for copy in copies:
        copy.start()
    rows = jnp.concatenate(_sum_rows(et_ref, True), axis=0)
    start = 0
    for a_ref in (a0, a1):
        for j in range(a_ref.shape[1] // 256):
            cols = slice(start + j * 256, start + (j + 1) * 256)
            out = jnp.dot(rows, a_ref[:, j * 256:(j + 1) * 256], preferred_element_type=F32)
            sent_ref[:, cols] = out[:256].astype(BF16)
            kept_ref[:, cols] = out[256:].astype(BF16)
        start += a_ref.shape[1]
    for copy in copies:
        copy.wait()


def _home(*inputs):
    return _kernel(
        _home_body, [_shape(256, 2048), _shape(256, 2048), _shape(2048, 2048)], inputs, "home",
        scratch=[pltpu.SemaphoreType.DMA((64,))], hbm_out=(2,), flops=1,
    )


def _fold_body(kept_ref, *refs):
    start = 0
    for ref in refs[:-1]:
        cols = slice(start, start + ref.shape[1])
        start += ref.shape[1]
        refs[-1][:, cols] = (kept_ref[:, cols].astype(F32) + ref[...].astype(F32)).astype(BF16)


def _fold(kept, *sent):
    return _kernel(_fold_body, [_shape(*kept.shape)], [kept, *sent], "fold", flops=1)[0]


def _fold_mass_body(mass_ref, other_ref, *refs):
    _fold_body(*refs[:-1])
    refs[-1][...] = mass_ref[...] + other_ref[...]


def _fold_mass(mass, other, kept, *sent):
    outs = [_shape(*kept.shape), _shape(1, 2048, dtype=F32)]
    return _kernel(_fold_mass_body, outs, [mass, other, kept, *sent], "fold", flops=1)


def _base_body(in_ref, home_ref, previous_ref, out_ref):
    width = in_ref.shape[1]
    for n in range(0, 2048, 256):
        cols = slice(n, n + 256)
        value = home_ref[:, cols].astype(F32) + PRIOR * previous_ref[:, cols].astype(F32)
        if n < width:
            value = value + in_ref[:, cols].astype(F32)
        out_ref[:, cols] = value


def _base(*inputs):
    return _kernel(_base_body, [_shape(256, 2048, dtype=F32)], inputs, "base", flops=2**36)[0]


def _final_body(base_ref, in_ref, sent_ref, mass_ref, other_ref, out_ref, total_ref, result, sem):
    total = mass_ref[...] + other_ref[...]
    total_ref[...] = total
    inverse = 1.0 / (total + PRIOR)
    start = 2048 - in_ref.shape[1]
    copies = []
    for n in range(4):
        rows = slice(n * 64, (n + 1) * 64)
        head = base_ref[rows, :start] + sent_ref[rows, :start].astype(F32)
        result[rows, :start] = (head * inverse[:, :start]).astype(BF16)
        rest = base_ref[rows, start:] + sent_ref[rows, start:].astype(F32) + in_ref[rows, :].astype(F32)
        result[rows, start:] = (rest * inverse[:, start:]).astype(BF16)
        copies.append(pltpu.make_async_copy(
            result.at[pl.ds(n * 64, 64)], out_ref.at[pl.ds(n * 64, 64)], sem.at[n]
        ))
        copies[-1].start()
    for copy in copies:
        copy.wait()


def _final(*inputs):
    return _kernel(
        _final_body, [_shape(256, 2048), _shape(1, 2048, dtype=F32)], inputs, "final",
        scratch=[pltpu.VMEM((256, 2048), BF16), pltpu.SemaphoreType.DMA((4,))], hbm_out=(0,),
    )


def on_device(embeddings, centroids):
    other = _copy(_send(embeddings, FAR))
    own = [embeddings] + [_send(embeddings, _first(-k)) for k in (1, 2, 3)]
    other = [other] + [_send(other, _first(-k)) for k in (1, 2, 3)]
    c = centroids
    own, other = lax.optimization_barrier((own, other))
    e0a = _join(own[0], other[0], own[1], other[1])
    e0b = _join(own[2], other[2], own[3], other[3])
    e3b, e1a = _send(e0b, _second(1)), _send(e0a, _second(-1))
    e3a, e1b = _send(e0a, _second(1)), _send(e0b, _second(-1))
    calls = [_soft([e0a, e0b], (0, 1), c, None)]
    previous, et = calls[0][4][0], calls[0][3]
    e3b, e1a, et = lax.optimization_barrier((e3b, e1a, et))
    e2b, e2a = _send(e3b, _second(1)), _send(e1a, _second(-1))
    calls.append(_soft([e3b, e1a], (7, 2), c, et))
    calls.append(_soft([e3a, e1b], (6, 3), c, calls[1][3]))
    calls.append(_soft([e2a, e2b], (4, 5), c, calls[2][3]))
    et = calls[3][3]

    probs, where = [None] * 8, [None] * 16
    for n, (call, slots) in enumerate(zip(calls, ((0, 1), (7, 2), (6, 3), (4, 5)))):
        for i, slot in enumerate(slots):
            probs[slot] = call[0][i]
            where[2 * slot], where[2 * slot + 1] = (n, 2 * i), (n, 2 * i + 1)
    peaks = [call[1] for call in calls]
    parts = _pack([call[2] for call in calls], where)
    total = _merge(lax.all_to_all(parts, "cent", 0, 0).reshape(32, 16, 128))

    a0, sent, kept, mass = _assign(where, 0, HEAD, probs, peaks, total, et)
    out0 = _fold(kept, *(lax.ppermute(part, "dp", CORE) for part in sent))
    out0, total = lax.optimization_barrier((out0, total))
    in0 = lax.ppermute(out0, "dp", NEAR)
    a1, sent, kept, mass = _assign(where, sum(HEAD), REST, probs, peaks, total, et, mass)
    other_mass = lax.ppermute(mass, "dp", CORE)
    out1, mass = _fold_mass(mass, other_mass, kept, *(lax.ppermute(part, "dp", CORE) for part in sent))
    in1 = _copy(lax.ppermute(out1, "dp", NEAR))
    a0, out1 = lax.optimization_barrier((a0, out1))
    sent, kept, placed = _home(et, a0, a1)
    base, sent = lax.optimization_barrier((_base(in0, kept, previous), sent))
    sent = lax.ppermute(sent, "dp", CORE)
    result, mass = _final(base, in1, sent, mass, lax.ppermute(mass, "dp", NEAR))
    return placed, mass.reshape(2048), result


def solution(mesh):
    placed = (P(("dp", "cent"), None), P("cent", None))
    return jax.shard_map(
        on_device,
        mesh=mesh,
        in_specs=placed,
        out_specs=(P("dp", "cent"), P("cent"), P("dp", "cent")),
        check_vma=False,
    )
```

```python
import functools
import math

import jax
import jax.numpy as jnp
from jax import lax
from jax.experimental import pallas as pl
from jax.experimental.pallas import tpu as pltpu
from jax.sharding import PartitionSpec as P

TEMP_INV = 2.0
PRIOR = 0.05
SCALE = TEMP_INV * math.log2(math.e)
AXES = ("dp", "cent")
VMEM = pl.BlockSpec(memory_space=pltpu.VMEM)
HBM = pl.BlockSpec(memory_space=pltpu.HBM)
HEAD, REST = (768,), (512, 512, 256)
LIMIT = 16 * 2**20
F32, BF16 = jnp.float32, jnp.bfloat16


def _perm(move):
    pairs = []
    for dp in range(4):
        for cent in range(32):
            core = dp & 1
            far, x, z = cent >> 4, (cent >> 2) & 3, cent & 3
            first, second = (z, x) if core == 0 else (x, z)
            far, first, second = move(far, first, second)
            x, z = (second, first) if core == 0 else (first, second)
            pairs.append((dp * 32 + cent, dp * 32 + (far % 2) * 16 + (x % 4) * 4 + z % 4))
    return pairs


def _first(k):
    return _perm(lambda h, a, b: (h, a + k, b))


def _second(k):
    return _perm(lambda h, a, b: (h, a, b + k))


FAR = _perm(lambda h, a, b: (h + 1, a, b))
CORE = [(i, i ^ 1) for i in range(4)]
NEAR = [(i, i ^ 2) for i in range(4)]


def _send(value, pairs):
    return lax.ppermute(value, AXES, pairs)


def _shape(*dims, dtype=BF16):
    return jax.ShapeDtypeStruct(dims, dtype)


def _kernel(body, outs, inputs, name, scratch=(), hbm_in=(), hbm_out=(), aliases=None, limit=LIMIT, flops=0):
    return pl.pallas_call(
        body,
        out_shape=outs,
        in_specs=[HBM if i in hbm_in else VMEM for i in range(len(inputs))],
        out_specs=[HBM if i in hbm_out else VMEM for i in range(len(outs))],
        scratch_shapes=list(scratch),
        input_output_aliases=aliases or {},
        compiler_params=pltpu.CompilerParams(vmem_limit_bytes=limit),
        cost_estimate=pl.CostEstimate(flops=flops, bytes_accessed=0, transcendentals=0) if flops else None,
        name=name,
    )(*inputs)


def _place_of(a, b):
    core, cent = lax.axis_index("dp") & 1, lax.axis_index("cent")
    x, z = (cent >> 2) & 3, cent & 3
    first = (jnp.where(core == 0, z, x) + a) & 3
    second = (jnp.where(core == 0, x, z) + b) & 3
    return jnp.where(core == 0, second, first) * 4 + jnp.where(core == 0, first, second)


def _far():
    return lax.axis_index("cent") >> 4


def _swap_far(row):
    return jnp.where(_far() == 0, row, pltpu.roll(row, 64, axis=1))


def _join_body(*refs):
    start = 0
    for ref in refs[:-1]:
        refs[-1][start:start + ref.shape[0], :] = ref[...]
        start += ref.shape[0]


def _join(*parts):
    rows = sum(p.shape[0] for p in parts)
    return _kernel(_join_body, [_shape(rows, 1024)], parts, "join")[0]


def _soft_body(n, slots, first, *refs):
    e_refs, c_ref, refs = refs[:n], refs[n], refs[n + (1 if first else 2):]
    p_refs, (peak_ref, part_ref, et_ref, *previous, lg) = refs[:n], refs[n:]
    if first:
        width = previous[0].shape[0]
        offset = pl.multiple_of(lax.axis_index("dp") * width, width)
        previous[0][...] = jnp.transpose(c_ref[:, pl.ds(offset, width)])
    for i in range(n):
        e = e_refs[i][...]
        et_ref[:, slots[i] * 256:(slots[i] + 1) * 256] = jnp.transpose(e)
        top = None
        for j in range(4):
            part = lax.dot_general(
                e, c_ref[j * 512:(j + 1) * 512, :], (((1,), (1,)), ((), ())),
                preferred_element_type=F32,
            )
            lg[:, j * 512:(j + 1) * 512] = part
            for q in range(4):
                piece = part[:, q * 128:(q + 1) * 128]
                top = piece if top is None else jnp.maximum(top, piece)
        peak = jnp.max(top, axis=1, keepdims=True)
        total = None
        for j in range(16):
            cols = slice(j * 128, (j + 1) * 128)
            value = jnp.exp2((lg[:, cols] - peak) * SCALE)
            total = value if total is None else total + value
            p_refs[i][:, cols] = value
        total = jnp.sum(total, axis=1, keepdims=True)
        peak = jnp.transpose(jnp.broadcast_to(peak * SCALE, (256, 128)))
        total = jnp.transpose(jnp.broadcast_to(total, (256, 128)))
        for q in range(2):
            lanes = slice(q * 128, (q + 1) * 128)
            row = slice(i * 2 + q, i * 2 + q + 1)
            peak_ref[row, :] = peak[:1, lanes]
            part_ref[row, :] = peak[:1, lanes] + jnp.log2(total[:1, lanes])


def _soft(pieces, slots, c, et):
    n, first = len(pieces), et is None
    stat = _shape(2 * n, 128, dtype=F32)
    outs = [_shape(256, 2048, dtype=F32)] * n + [stat, stat, _shape(1024, 2048)]
    scratch = [pltpu.VMEM((256, 2048), F32)]
    body = functools.partial(_soft_body, n, slots, first)
    inputs, aliases = ([*pieces, c], None) if first else ([*pieces, c, et], {n + 1: n + 2})
    if first:
        outs.append(_shape(256, 2048))
    outs = _kernel(body, outs, inputs, "soft", scratch=scratch, aliases=aliases)
    return outs[:n], outs[n], outs[n + 1], outs[n + 2], outs[n + 3:]


def _pack_body(where, *refs):
    out_ref, one = refs[-2], refs[-1]
    for b in range(4):
        for a in range(4):
            call, i = where[b * 4 + a]
            one[pl.ds(_place_of(a, b), 1), :] = _swap_far(refs[call][i:i + 1, :])
    packed = one[...]
    for i in range(32):
        out_ref[i] = packed


def _pack(parts, where):
    return _kernel(
        functools.partial(_pack_body, where), [_shape(32, 16, 128, dtype=F32)], parts, "pack",
        scratch=[pltpu.VMEM((16, 128), F32)],
    )[0]


def _merge_body(in_ref, out_ref):
    values = [in_ref[i] for i in range(32)]
    top = functools.reduce(jnp.maximum, values)
    out_ref[...] = top + jnp.log2(sum(jnp.exp2(v - top) for v in values))


def _merge(values):
    return _kernel(_merge_body, [_shape(16, 128, dtype=F32)], [values], "merge")[0]


def _copy_body(in_ref, out_ref):
    out_ref[...] = in_ref[...]


def _copy(value):
    return _kernel(_copy_body, [_shape(*value.shape)], [value], "copy", flops=2**36)[0]


def _sum_rows(et_ref, home):
    dp = lax.axis_index("dp")
    near, core = dp >> 1, dp & 1
    base = (near if home else 1 - near) * 512
    sent = et_ref[pl.ds(pl.multiple_of(base + (1 - core) * 256, 256), 256), :]
    kept = et_ref[pl.ds(pl.multiple_of(base + core * 256, 256), 256), :]
    return [sent, kept]


def _assign_dot(where, start, width, p_refs, peaks, total_ref, scale_ref, a_ref, rows, store):
    for g in range(16):
        call, i = where[g]
        row = peaks[call][i:i + 1, :] - _swap_far(total_ref[pl.ds(_place_of(g % 4, g // 4), 1), :])
        scale_ref[g * 128:(g + 1) * 128, :] = jnp.transpose(jnp.broadcast_to(jnp.exp2(row), (128, 128)))
    for n in range(width // 256):
        for g in range(16):
            scale = scale_ref[g * 128:(g + 1) * 128, :]
            for j in range(2 * n, 2 * n + 2):
                value = p_refs[g // 2][g % 2 * 128:(g % 2 + 1) * 128, start + j * 128:start + (j + 1) * 128]
                a_ref[g * 128:(g + 1) * 128, j * 128:(j + 1) * 128] = (value * scale).astype(BF16)
        cols = slice(n * 256, (n + 1) * 256)
        store(n, cols, jnp.dot(rows, a_ref[:, cols], preferred_element_type=F32))


def _assign_body(where, start, width, parts, calls, *refs):
    p_refs, peaks, refs = refs[:8], refs[8:8 + calls], refs[8 + calls:]
    total_ref, et_ref = refs[:2]
    mass_in = refs[2] if start else None
    a_ref, *refs = refs[3:] if start else refs[2:]
    sent_refs, (kept_ref, mass_ref, scale_ref) = refs[:len(parts)], refs[len(parts):]
    rows = jnp.concatenate(_sum_rows(et_ref, False) + [jnp.ones((16, 2048), BF16)], axis=0)

    def store(n, cols, out):
        first, part = n * 256, 0
        while first >= parts[part]:
            first, part = first - parts[part], part + 1
        sent_refs[part][:, first:first + 256] = out[:256].astype(BF16)
        kept_ref[:, cols] = out[256:512].astype(BF16)
        mass_ref[:, start + n * 256:start + (n + 1) * 256] = out[512:513]

    _assign_dot(where, start, width, p_refs, peaks, total_ref, scale_ref, a_ref, rows, store)
    if start:
        mass_ref[:, :start] = mass_in[...]


def _assign(where, start, parts, ps, peaks, total, et, *mass):
    width, n = sum(parts), len(parts)
    outs = _kernel(
        functools.partial(_assign_body, where, start, width, parts, len(peaks)),
        [_shape(2048, width)] + [_shape(256, part) for part in parts]
        + [_shape(256, width), _shape(1, start + width, dtype=F32)],
        [*ps, *peaks, total, et, *mass], "assign", scratch=[pltpu.VMEM((2048, 128), F32)],
    )
    return outs[0], outs[1:1 + n], outs[1 + n], outs[2 + n]


def _home_body(et_ref, a0, a1, sent_ref, kept_ref, placed_ref, sem):
    copies = []
    for i in range(32):
        row = pl.multiple_of(((_far() ^ (i % 2)) * 16 + _place_of(i // 2 % 4, i // 8)) * 64, 64)
        start = 0
        for n, a_ref in enumerate((a0, a1)):
            copies.append(pltpu.make_async_copy(
                a_ref.at[pl.ds(i * 64, 64)],
                placed_ref.at[pl.ds(row, 64), pl.ds(start, a_ref.shape[1])],
                sem.at[2 * i + n],
            ))
            start += a_ref.shape[1]
    for copy in copies:
        copy.start()
    rows = jnp.concatenate(_sum_rows(et_ref, True), axis=0)
    start = 0
    for a_ref in (a0, a1):
        for j in range(a_ref.shape[1] // 256):
            cols = slice(start + j * 256, start + (j + 1) * 256)
            out = jnp.dot(rows, a_ref[:, j * 256:(j + 1) * 256], preferred_element_type=F32)
            sent_ref[:, cols] = out[:256].astype(BF16)
            kept_ref[:, cols] = out[256:].astype(BF16)
        start += a_ref.shape[1]
    for copy in copies:
        copy.wait()


def _home(*inputs):
    return _kernel(
        _home_body, [_shape(256, 2048), _shape(256, 2048), _shape(2048, 2048)], inputs, "home",
        scratch=[pltpu.SemaphoreType.DMA((64,))], hbm_out=(2,), flops=1,
    )


def _fold_body(kept_ref, *refs):
    start = 0
    for ref in refs[:-1]:
        cols = slice(start, start + ref.shape[1])
        start += ref.shape[1]
        refs[-1][:, cols] = (kept_ref[:, cols].astype(F32) + ref[...].astype(F32)).astype(BF16)


def _fold(kept, *sent):
    return _kernel(_fold_body, [_shape(*kept.shape)], [kept, *sent], "fold", flops=1)[0]


def _fold_mass_body(mass_ref, other_ref, *refs):
    _fold_body(*refs[:-1])
    refs[-1][...] = mass_ref[...] + other_ref[...]


def _fold_mass(mass, other, kept, *sent):
    outs = [_shape(*kept.shape), _shape(1, 2048, dtype=F32)]
    return _kernel(_fold_mass_body, outs, [mass, other, kept, *sent], "fold", flops=1)


def _base_body(in_ref, home_ref, previous_ref, out_ref):
    width = in_ref.shape[1]
    for n in range(0, 2048, 256):
        cols = slice(n, n + 256)
        value = home_ref[:, cols].astype(F32) + PRIOR * previous_ref[:, cols].astype(F32)
        if n < width:
            value = value + in_ref[:, cols].astype(F32)
        out_ref[:, cols] = value


def _base(*inputs):
    return _kernel(_base_body, [_shape(256, 2048, dtype=F32)], inputs, "base", flops=2**36)[0]


def _final_body(base_ref, in_ref, sent_ref, mass_ref, other_ref, out_ref, total_ref, result, sem):
    total = mass_ref[...] + other_ref[...]
    total_ref[...] = total
    inverse = 1.0 / (total + PRIOR)
    start = 2048 - in_ref.shape[1]
    copies = []
    for n in range(4):
        rows = slice(n * 64, (n + 1) * 64)
        head = base_ref[rows, :start] + sent_ref[rows, :start].astype(F32)
        result[rows, :start] = (head * inverse[:, :start]).astype(BF16)
        rest = base_ref[rows, start:] + sent_ref[rows, start:].astype(F32) + in_ref[rows, :].astype(F32)
        result[rows, start:] = (rest * inverse[:, start:]).astype(BF16)
        copies.append(pltpu.make_async_copy(
            result.at[pl.ds(n * 64, 64)], out_ref.at[pl.ds(n * 64, 64)], sem.at[n]
        ))
        copies[-1].start()
    for copy in copies:
        copy.wait()


def _final(*inputs):
    return _kernel(
        _final_body, [_shape(256, 2048), _shape(1, 2048, dtype=F32)], inputs, "final",
        scratch=[pltpu.VMEM((256, 2048), BF16), pltpu.SemaphoreType.DMA((4,))], hbm_out=(0,),
    )


def on_device(embeddings, centroids):
    other = _copy(_send(embeddings, FAR))
    own = [embeddings] + [_send(embeddings, _first(-k)) for k in (1, 2, 3)]
    other = [other] + [_send(other, _first(-k)) for k in (1, 2, 3)]
    c = centroids
    own, other = lax.optimization_barrier((own, other))
    e0a = _join(own[0], other[0], own[1], other[1])
    e0b = _join(own[2], other[2], own[3], other[3])
    e3b, e1a = _send(e0b, _second(1)), _send(e0a, _second(-1))
    e3a, e1b = _send(e0a, _second(1)), _send(e0b, _second(-1))
    calls = [_soft([e0a, e0b], (0, 1), c, None)]
    previous, et = calls[0][4][0], calls[0][3]
    e2b, e2a = _send(e3b, _second(1)), _send(e1a, _second(-1))
    e3b, e1a, et = lax.optimization_barrier((e3b, e1a, et))
    calls.append(_soft([e3b, e1a], (7, 2), c, et))
    calls.append(_soft([e3a, e1b], (6, 3), c, calls[1][3]))
    calls.append(_soft([e2a, e2b], (4, 5), c, calls[2][3]))
    et = calls[3][3]

    probs, where = [None] * 8, [None] * 16
    for n, (call, slots) in enumerate(zip(calls, ((0, 1), (7, 2), (6, 3), (4, 5)))):
        for i, slot in enumerate(slots):
            probs[slot] = call[0][i]
            where[2 * slot], where[2 * slot + 1] = (n, 2 * i), (n, 2 * i + 1)
    peaks = [call[1] for call in calls]
    parts = _pack([call[2] for call in calls], where)
    total = _merge(lax.all_to_all(parts, "cent", 0, 0).reshape(32, 16, 128))

    a0, sent, kept, mass = _assign(where, 0, HEAD, probs, peaks, total, et)
    out0 = _fold(kept, *(lax.ppermute(part, "dp", CORE) for part in sent))
    out0, total = lax.optimization_barrier((out0, total))
    in0 = lax.ppermute(out0, "dp", NEAR)
    a1, sent, kept, mass = _assign(where, sum(HEAD), REST, probs, peaks, total, et, mass)
    other_mass = lax.ppermute(mass, "dp", CORE)
    out1, mass = _fold_mass(mass, other_mass, kept, *(lax.ppermute(part, "dp", CORE) for part in sent))
    in1 = _copy(lax.ppermute(out1, "dp", NEAR))
    a0, out1 = lax.optimization_barrier((a0, out1))
    sent, kept, placed = _home(et, a0, a1)
    base, sent = lax.optimization_barrier((_base(in0, kept, previous), sent))
    sent = lax.ppermute(sent, "dp", CORE)
    result, mass = _final(base, in1, sent, mass, lax.ppermute(mass, "dp", NEAR))
    return placed, mass.reshape(2048), result


def solution(mesh):
    placed = (P(("dp", "cent"), None), P("cent", None))
    return jax.shard_map(
        on_device,
        mesh=mesh,
        in_specs=placed,
        out_specs=(P("dp", "cent"), P("cent"), P("dp", "cent")),
        check_vma=False,
    )
```
